256 devices in a mesh: rep: 32 (over x, z_lo, core), fsdp: 8 (over z_hi, y).
Axes of the slice: x: 4, y: 4, z: 8 (z_hi: 2, z_lo: 4; z = z_hi * 4 + z_lo), core: 2. Of those that a mesh axis runs over, the one named last changes fastest.
Arguments:
- tokens: bfloat16 [49152, 5120], P(('rep', 'fsdp')), may hold values from -6 to 6
- cotangent: bfloat16 [49152, 2560], P(('rep', 'fsdp')), may hold values from -0.15625 to 0.15625
- momentum: bfloat16 [32, 5120, 2560], P('rep', 'fsdp'), may hold values from -6 to 6
- positions: int32 [5120, 320], P('fsdp'), may hold values from 0 to 63, as said below
Outputs:
- new_momentum: bfloat16 [32, 5120, 2560], P('rep', 'fsdp')
- update: bfloat16 [5120, 2560], P(('fsdp', 'rep'))
The draws below stay inside these ranges and needn't reach their ends.
Inputs may be any that keep to these rules, and one draw needn't show every extreme that they name: The 8 positions of each block are distinct; the same positions hold for every replica.
All inputs are finite; a program needn't handle non-finite values.
Results may differ from the reference program's by a relative error of at most 0.015.
Values may be sent and summed in bfloat16 or wider, within the bound.
A program may use at most 128 MiB of HBM per device.

```python
import math
import jax
import jax.numpy as jnp
from jax import lax

D = 5120
SPAN = 64
KEEP = 8
F = 2560
NCHUNK = 40
REPLICAS = 32
REPLICA_TOKENS = 1536
TOKENS = 49152


def draw_positions(key, part):
    key = jax.random.fold_in(key, 7)
    scores = jax.random.randint(key, (D, F // SPAN, SPAN), 0, 1 << 20) * SPAN + jnp.arange(SPAN, dtype=jnp.int32)
    ranking = jnp.argsort(scores, axis=-1)
    return ranking[..., :KEEP].reshape(D, F // SPAN * KEEP).astype(jnp.int32)


def shard_levels(own_key, shape, shards, least, largest):
    loudness = 1.0
    for position, blocks in shards:
        heights = jax.random.uniform(jax.random.fold_in(jax.random.fold_in(own_key, 6), position), (blocks,), jnp.float32, least / len(shards), largest / len(shards))
        loudness = loudness * jnp.repeat(jnp.exp(heights), shape[position] // blocks).reshape((-1,) + (1,) * (len(shape) - 1 - position))
    return loudness


def noise(own_key, dims, scale, most, cuts=(), held_as=jnp.bfloat16):
    entries = jax.random.normal(own_key, dims, jnp.float32) * scale
    if len(cuts) > 0:
        entries = shard_levels(own_key, dims, cuts, -0.22, 0.18) * entries
    return jnp.clip(entries, min=-most, max=most).astype(held_as)


def setup_inputs(seed: int = 0) -> dict:
    key_of = jax.random.split(jax.random.key(seed), 5)
    return {
        "tokens": noise(key_of[0], (TOKENS, D), 1.0, 6.0, ((0, 256),)),
        "cotangent": noise(key_of[1], (TOKENS, F), REPLICA_TOKENS ** -0.5, 0.15625, ((0, 256),)),
        "momentum": noise(key_of[2], (REPLICAS, D, F), 1.0, 6.0, ((0, 32), (1, 8))),
        "positions": draw_positions(jax.random.fold_in(key_of[4], 71), 0),
    }


momentum_decay = 0.9

def dct_basis(length):
    freqs = jnp.arange(length, dtype=jnp.float32)[:, None]
    places = jnp.arange(length, dtype=jnp.float32)[None, :]
    weights = jnp.where(freqs == 0.0, math.sqrt(1.0 / length), math.sqrt(2.0 / length))
    return (weights * jnp.cos(math.pi * (2.0 * places + 1.0) * freqs / (2.0 * length))).astype(jnp.float32)

def selection(slots, length, keep):
    rows = slots.shape[0]
    grouped = slots.reshape(rows, -1, keep)
    return grouped[..., None] == jnp.arange(length, dtype=jnp.int32)

def expand(values, chosen, basis):
    spread = lax.optimization_barrier(jnp.sum(jnp.where(chosen, values[..., None], 0.0), axis=2))
    return jnp.einsum('rck,kj->rcj', spread, basis, precision=lax.Precision.HIGHEST)

def compress(updated, slots, basis, keep):
    rows, width = updated.shape
    length = basis.shape[0]
    spans = updated.reshape(rows, width // length, length)
    coeffs = jnp.einsum('rcj,kj->rck', spans, basis, precision=lax.Precision.HIGHEST)
    chosen = selection(slots, length, keep)
    values = lax.optimization_barrier(jnp.sum(jnp.where(chosen, coeffs[:, :, None, :], 0.0), axis=3)).astype(jnp.bfloat16)
    restored = expand(values.astype(jnp.float32), chosen, basis)
    leftover = (spans - restored).reshape(rows, width).astype(jnp.bfloat16)
    return (values.reshape(rows, -1), leftover)

def decode(summed, slots, basis, keep, factor):
    rows = summed.shape[0]
    length = basis.shape[0]
    chosen = selection(slots, length, keep)
    restored = expand(summed.reshape(rows, -1, keep), chosen, basis)
    return (restored.reshape(rows, -1) * factor).astype(jnp.bfloat16)

def reference(tokens, cotangent, momentum, positions):
    basis = dct_basis(SPAN)
    token_groups = tokens.reshape(REPLICAS, REPLICA_TOKENS, D)
    cot_groups = cotangent.reshape(REPLICAS, REPLICA_TOKENS, F)

    def replica_step(summed, inputs):
        group_tokens, group_cot, previous = inputs
        gradient = jnp.dot(group_tokens.T, group_cot, preferred_element_type=jnp.float32)
        updated = momentum_decay * previous.astype(jnp.float32) + gradient
        values, leftover = compress(updated, positions, basis, KEEP)
        return (summed + values.astype(jnp.float32), leftover)
    initial = jnp.zeros((D, NCHUNK * KEEP), jnp.float32)
    summed, new_momentum = lax.scan(replica_step, initial, (token_groups, cot_groups, momentum))
    update = decode(summed, positions, basis, KEEP, 1.0 / math.sqrt(REPLICAS))
    return (new_momentum, update)
```

```python
import functools
import math

import jax
import jax.numpy as jnp
import numpy as np
from jax import lax
from jax.experimental import pallas as pl
from jax.experimental.pallas import tpu as pltpu
from jax.sharding import PartitionSpec as P

SPAN = 64
KEEP = 8
MOMENTUM_DECAY = 0.9
MESH = pl.DeviceIdType.MESH

REPLICAS = 32
ROWS = 640
WIDTH = 2560
BLOCK = 192
SLOTS = 8
PIECE = 256
PIECES = WIDTH // PIECE
GROUPS = 3
GROUP_ROWS = ROWS // 4
WINDOW = 32
AHEAD = 3


def block_bases():
    freqs = np.arange(SPAN, dtype=np.float64)[:, None]
    places = np.arange(SPAN, dtype=np.float64)[None, :]
    weights = np.where(freqs == 0.0, math.sqrt(1.0 / SPAN), math.sqrt(2.0 / SPAN))
    basis = (weights * np.cos(math.pi * (2.0 * places + 1.0) * freqs / (2.0 * SPAN))).astype(np.float32)
    inverse = np.kron(np.eye(PIECE // SPAN, dtype=np.float32), basis)
    out = []
    for matrix in (inverse.T, inverse):
        high = matrix.astype(jnp.bfloat16)
        low = (matrix - high.astype(np.float32)).astype(jnp.bfloat16)
        out += [high, low]
    return np.stack(out)


def split(value):
    high = value.astype(jnp.bfloat16)
    return high, (value - high.astype(jnp.float32)).astype(jnp.bfloat16)


def mm(a, b):
    return jnp.dot(a, b, preferred_element_type=jnp.float32)


def lane_gather(value, index):
    return jnp.take_along_axis(value, index, axis=1, mode="promise_in_bounds")


ZT, ZG = 0, 4
YT, YTP = 14, 17
YG, YGR = 20, 22
YP, YPR = 24, 24 + 2 * PIECES
A0 = 24 + 4 * PIECES
B0 = A0 + 3 * GROUPS
REMOTE = B0 + 7 * GROUPS


def kernel(
    tok, cot, mom, pos, bases, out, upd,
    tall, gall, relay, tt, mom_s, pos_s, mask_s, idx_s, gidx_s, out_s, upd_s, vals_f, vals_b, abuf, pbuf, bbuf,
    ss, rs, ls,
):
    rep = lax.axis_index("rep")
    f = lax.axis_index("fsdp")
    x, q = rep // 8, lax.rem(rep, 8)
    zh, y = f // 4, lax.rem(f, 4)

    def at_y(j):
        return (rep, zh * 4 + lax.rem(y + j, 4))

    partner = (rep, lax.rem(f + 4, 8))

    def at_x(j):
        return (lax.rem(x + j, 4) * 8 + q, f)

    def at_q(j):
        return (x * 8 + lax.rem(q + j, 8), f)

    def remote(src, dst, k, device):
        return pltpu.make_async_remote_copy(
            src_ref=src, dst_ref=dst, send_sem=ss.at[k], recv_sem=rs.at[k], device_id=device, device_id_type=MESH
        )

    def tok_cols(block):
        return tok.at[:, pl.ds(pl.multiple_of(block * ROWS, 128), ROWS)]

    def cols(t):
        return pl.ds(pl.multiple_of(t * PIECE, PIECE), PIECE)

    def z_tok(j):
        src = tok_cols((1 - zh) * 4 + lax.rem(y + j, 4))
        return remote(src, tall.at[4] if j == 0 else relay.at[j - 1], ZT + j, partner)

    def z_cot(t):
        return remote(cot.at[:, cols(t)], gall.at[4, :, cols(t)], ZG + t, partner)

    def y_tok(j):
        return remote(tok_cols(zh * 4 + lax.rem(y + j, 4)), tall.at[4 - j], YT + j - 1, at_y(j))

    def y_tok_partner(j):
        return remote(relay.at[j - 1], tall.at[8 - j], YTP + j - 1, at_y(j))

    def y_cot(way):
        return remote(cot, gall.at[3 - 2 * way], YG + way, at_y(1 + 2 * way))

    def y_cot_relay(way):
        half = pl.ds(96 * way, 96)
        return remote(gall.at[3 - 2 * way, half], gall.at[2, half], YGR + way, at_y(1 + 2 * way))

    def y_piece(t, way):
        return remote(gall.at[4, :, cols(t)], gall.at[7 - 2 * way, :, cols(t)], YP + 2 * t + way, at_y(1 + 2 * way))

    def y_piece_relay(t, way):
        half = pl.ds(96 * way, 96)
        return remote(
            gall.at[7 - 2 * way, half, cols(t)], gall.at[6, half, cols(t)], YPR + 2 * t + way, at_y(1 + 2 * way)
        )

    def rep_x(b, j):
        rows = pl.ds(pl.multiple_of(lax.rem(x + j, 4) * GROUP_ROWS, 32), GROUP_ROWS)
        return remote(vals_b.at[b, rows], abuf.at[b, j - 1], A0 + 3 * b + j - 1, at_x(j))

    def window(who):
        return pl.ds(pl.multiple_of(((5 * who) // 4) * 16, 16), WINDOW)

    def rep_q(b, j):
        rows = window(lax.rem(q + j, 8))
        return remote(pbuf.at[b, rows], bbuf.at[b, j - 1], B0 + 7 * b + j - 1, at_q(j))

    def local(src, dst, k):
        return pltpu.make_async_copy(src, dst, ls.at[k])

    locals_in = [
        local(pos, pos_s, 0),
        local(cot, gall.at[0], 1),
        local(tok_cols(f), tall.at[0], 2),
        local(mom, mom_s, 3),
    ]
    for copy in locals_in:
        copy.start()

    barrier = pltpu.get_barrier_semaphore()
    friends = [partner] + [at_y(j) for j in (1, 2, 3)] + [at_x(j) for j in (1, 2, 3)] + [at_q(j) for j in range(1, 8)]
    for friend in friends:
        pl.semaphore_signal(barrier, inc=1, device_id=friend, device_id_type=MESH)
    pl.semaphore_wait(barrier, len(friends))

    for j in (1, 2, 3):
        z_tok(j).start()
    for way in (0, 1):
        y_cot(way).start()
    for j in (1, 3, 2):
        y_tok(j).start()

    locals_in[0].wait()

    def lanes(rows):
        return lax.broadcasted_iota(jnp.int32, (rows, 128), 1)

    def position_blocks(p):
        return (p[:, 0:128], p[:, 128:256], p[:, 192:320])

    def blocks_of(b):
        return [(bb, 8 * b + bb) for bb in range(8)] if b < 2 else [(bb, 12 + bb) for bb in range(4, 8)]

    def prepare(i, carry):
        rows = pl.ds(pl.multiple_of(i * 32, 32), 32)
        lane = lanes(32)
        half = 8 * (lane // 64)
        inside = lax.rem(lane, 64)
        shift = 64 * lax.rem(lane // 8, 2)
        for b, block in enumerate(position_blocks(pos_s[rows, :])):
            idx_s[b, rows, :] = block + shift
            for bb, column in blocks_of(b):
                hit = jnp.zeros((32, 128), jnp.float32)
                for m in range(KEEP):
                    hit = jnp.where(lane_gather(block, half + (16 * bb + m)) == inside, 1.0, hit)
                mask_s[rows, column * 128 : column * 128 + 128] = hit.astype(jnp.bfloat16)
        return carry

    lax.fori_loop(0, ROWS // 32, prepare, 0)

    lane32 = lanes(WINDOW)
    half32 = 8 * (lane32 // 64)
    inside32 = lax.rem(lane32, 64)
    for b, block in enumerate(position_blocks(pos_s[window(rep), :])):
        for bb, column in blocks_of(b):
            found = jnp.full((WINDOW, 128), -1, jnp.int32)
            for m in range(KEEP):
                source = half32 + (16 * bb + m)
                found = jnp.where(lane_gather(block, source) == inside32, source, found)
            gidx_s[:, column * 128 : column * 128 + 128] = found

    z_tok(1).wait_recv()
    y_tok_partner(1).start()
    z_tok(0).start()
    for way in (0, 1):
        y_cot(way).wait_recv()
        y_cot_relay(way).start()
    z_tok(2).wait_recv()
    y_tok_partner(2).start()
    z_cot(0).start()
    z_tok(3).wait_recv()
    y_tok_partner(3).start()
    z_cot(1).start()

    def turn(pair):
        block = tall[2 * pair : 2 * pair + 2].reshape(2 * BLOCK, ROWS)
        tt[:, pair * 2 * BLOCK : (pair + 1) * 2 * BLOCK] = block.T

    for copy in locals_in[1:]:
        copy.wait()
    for j in (1, 2, 3):
        y_tok(j).wait_recv()
    turn(0)
    turn(1)
    z_tok(0).wait_recv()
    z_cot(2).start()
    for j in (1, 2, 3):
        y_tok_partner(j).wait_recv()
    turn(2)
    turn(3)
    for way in (0, 1):
        y_cot_relay(way).wait_recv()

    def compute(s):
        c = cols(s)
        gradient = mm(tt[...], gall[:, :, c].reshape(SLOTS * BLOCK, PIECE))
        updated = MOMENTUM_DECAY * mom_s[:, c].astype(jnp.float32) + gradient
        high, low = split(updated)
        coeffs = mm(high, bases[0]) + mm(low, bases[0]) + mm(high, bases[1])
        rounded = coeffs.astype(jnp.bfloat16)
        kept = rounded * mask_s[:, c]
        restored = mm(kept, bases[2]) + mm(kept, bases[3])
        out_s[s] = (updated - restored).astype(jnp.bfloat16)
        local(out_s.at[s], out.at[:, c], 4 + s).start()
        b = s // 4
        first = 2 * lax.rem(s, 4) + jnp.where(s >= 8, 4, 0)
        index = idx_s[b]
        values = vals_f[...]
        place = lanes(ROWS) // 16
        wide = rounded.astype(jnp.float32)
        for k in (0, 1):
            values = jnp.where(place == first + k, lane_gather(wide[:, k * 128 : k * 128 + 128], index), values)
        vals_f[...] = values

    def share(b):
        vals_b[b] = vals_f[...].astype(jnp.bfloat16)
        for j in (1, 2, 3):
            rep_x(b, j).start()

    def add_x(b):
        own = pl.ds(pl.multiple_of(x * GROUP_ROWS, 32), GROUP_ROWS)
        total = vals_b[b, own, :].astype(jnp.float32)
        for j in (1, 2, 3):
            rep_x(b, j).wait_recv()
            total = total + abuf[b, j - 1].astype(jnp.float32)
        pbuf[b] = total
        for j in range(1, 8):
            rep_q(b, j).start()

    def decode(b):
        total = pbuf[b, window(q), :]
        for j in range(1, 8):
            rep_q(b, j).wait_recv()
            total = total + bbuf[b, j - 1]
        parts = []
        for _, column in blocks_of(b):
            found = gidx_s[:, column * 128 : column * 128 + 128]
            parts.append(jnp.where(found >= 0, lane_gather(total, jnp.maximum(found, 0)), 0.0))
        spread = jnp.concatenate(
            [jnp.concatenate(parts[k : k + 2], axis=1) for k in range(0, len(parts), 2)], axis=0
        )
        high, low = split(spread)
        restored = mm(high, bases[2]) + mm(low, bases[2]) + mm(high, bases[3])
        restored = (restored * (1.0 / math.sqrt(REPLICAS))).astype(jnp.bfloat16)
        for k in range(len(parts) // 2):
            upd_s[:, b * 1024 + k * PIECE : b * 1024 + (k + 1) * PIECE] = restored[k * WINDOW : (k + 1) * WINDOW]

    vals_f[...] = jnp.zeros_like(vals_f)

    def step(t, carry):
        @pl.when(t < PIECES)
        def _():
            z_cot(t).wait_recv()
            for way in (0, 1):
                y_piece(t, way).start()

        @pl.when(t + AHEAD < PIECES)
        def _():
            z_cot(t + AHEAD).start()

        @pl.when((t >= 1) & (t <= PIECES))
        def _():
            for way in (0, 1):
                y_piece(t - 1, way).wait_recv()
                y_piece_relay(t - 1, way).start()

        @pl.when(t >= 2)
        def _():
            for way in (0, 1):
                y_piece_relay(t - 2, way).wait_recv()
            compute(t - 2)

        @pl.when(t == 5)
        def _():
            share(0)

        @pl.when(t == 7)
        def _():
            add_x(0)

        @pl.when(t == 9)
        def _():
            share(1)
            decode(0)

        return carry

    lax.fori_loop(0, PIECES + 2, step, 0)
    share(2)
    add_x(1)
    add_x(2)
    decode(1)
    decode(2)
    last = local(upd_s, upd, 4 + PIECES)
    last.start()

    for j in range(4):
        z_tok(j).wait_send()
    for j in (1, 2, 3):
        y_tok(j).wait_send()
        y_tok_partner(j).wait_send()
    for way in (0, 1):
        y_cot(way).wait_send()
        y_cot_relay(way).wait_send()

    def finish(t, carry):
        z_cot(t).wait_send()
        for way in (0, 1):
            y_piece(t, way).wait_send()
            y_piece_relay(t, way).wait_send()
        local(out_s.at[t], out.at[:, cols(t)], 4 + t).wait()
        return carry

    lax.fori_loop(0, PIECES, finish, 0)
    for b in range(GROUPS):
        for j in (1, 2, 3):
            rep_x(b, j).wait_send()
        for j in range(1, 8):
            rep_q(b, j).wait_send()
    last.wait()


def body(tokens, cotangent, momentum, positions):
    anywhere = pl.BlockSpec(memory_space=pl.ANY)
    bf16, f32, i32 = jnp.bfloat16, jnp.float32, jnp.int32
    new_momentum, update = pl.pallas_call(
        kernel,
        out_shape=(jax.ShapeDtypeStruct((ROWS, WIDTH), bf16), jax.ShapeDtypeStruct((WINDOW, WIDTH), bf16)),
        in_specs=[anywhere] * 4 + [pl.BlockSpec(memory_space=pltpu.VMEM)],
        out_specs=(anywhere, anywhere),
        scratch_shapes=[
            pltpu.VMEM((SLOTS, BLOCK, ROWS), bf16),
            pltpu.VMEM((SLOTS, BLOCK, WIDTH), bf16),
            pltpu.VMEM((3, BLOCK, ROWS), bf16),
            pltpu.VMEM((ROWS, SLOTS * BLOCK), bf16),
            pltpu.VMEM((ROWS, WIDTH), bf16),
            pltpu.VMEM((ROWS, WIDTH // SPAN * KEEP), i32),
            pltpu.VMEM((ROWS, WIDTH), bf16),
            pltpu.VMEM((GROUPS, ROWS, 128), i32),
            pltpu.VMEM((WINDOW, WIDTH), i32),
            pltpu.VMEM((PIECES, ROWS, PIECE), bf16),
            pltpu.VMEM((WINDOW, WIDTH), bf16),
            pltpu.VMEM((ROWS, 128), f32),
            pltpu.VMEM((GROUPS, ROWS, 128), bf16),
            pltpu.VMEM((GROUPS, 3, GROUP_ROWS, 128), bf16),
            pltpu.VMEM((GROUPS, GROUP_ROWS, 128), f32),
            pltpu.VMEM((GROUPS, 7, WINDOW, 128), f32),
            pltpu.SemaphoreType.DMA((REMOTE,)),
            pltpu.SemaphoreType.DMA((REMOTE,)),
            pltpu.SemaphoreType.DMA((5 + PIECES,)),
        ],
        compiler_params=pltpu.CompilerParams(
            collective_id=0, has_side_effects=True, vmem_limit_bytes=60 * 1024 * 1024
        ),
    )(tokens, cotangent, momentum.reshape(ROWS, WIDTH), positions, jnp.asarray(block_bases()))
    first = 4 * lax.rem(lax.axis_index("rep"), 4)
    update = lax.dynamic_slice_in_dim(update, first, ROWS // REPLICAS, 0)
    return new_momentum.reshape(1, ROWS, WIDTH), update


def solution(mesh):
    in_specs = (
        P(("rep", "fsdp"), None),
        P(("rep", "fsdp"), None),
        P("rep", "fsdp", None),
        P("fsdp", None),
    )
    out_specs = (P("rep", "fsdp", None), P(("fsdp", "rep"), None))
    return jax.shard_map(body, mesh=mesh, in_specs=in_specs, out_specs=out_specs, check_vma=False)
```

```python
import functools
import math

import jax
import jax.numpy as jnp
import numpy as np
from jax import lax
from jax.experimental import pallas as pl
from jax.experimental.pallas import tpu as pltpu
from jax.sharding import PartitionSpec as P

SPAN = 64
KEEP = 8
MOMENTUM_DECAY = 0.9
MESH = pl.DeviceIdType.MESH

REPLICAS = 32
ROWS = 640
WIDTH = 2560
BLOCK = 192
SLOTS = 8
PIECE = 256
PIECES = WIDTH // PIECE
WHOLE = PIECES - 1
HALF = PIECE // 2
GROUPS = 3
GROUP_ROWS = ROWS // 4
WINDOW = 32
AHEAD = 3


def block_bases():
    freqs = np.arange(SPAN, dtype=np.float64)[:, None]
    places = np.arange(SPAN, dtype=np.float64)[None, :]
    weights = np.where(freqs == 0.0, math.sqrt(1.0 / SPAN), math.sqrt(2.0 / SPAN))
    basis = (weights * np.cos(math.pi * (2.0 * places + 1.0) * freqs / (2.0 * SPAN))).astype(np.float32)
    inverse = np.kron(np.eye(PIECE // SPAN, dtype=np.float32), basis)
    out = []
    for matrix in (inverse.T, inverse):
        high = matrix.astype(jnp.bfloat16)
        low = (matrix - high.astype(np.float32)).astype(jnp.bfloat16)
        out += [high, low]
    return np.stack(out)


def split(value):
    high = value.astype(jnp.bfloat16)
    return high, (value - high.astype(jnp.float32)).astype(jnp.bfloat16)


def mm(a, b):
    return jnp.dot(a, b, preferred_element_type=jnp.float32)


def lane_gather(value, index):
    return jnp.take_along_axis(value, index, axis=1, mode="promise_in_bounds")


ZT, ZG, ZH = 0, 4, 4 + WHOLE
YT = ZH + 2
YTP, YG, YGR = YT + 3, YT + 6, YT + 8
YP = YGR + 2
YPR = YP + 2 * WHOLE
YH = YPR + 2 * WHOLE
A0 = YH + 6
B0 = A0 + 3 * GROUPS
REMOTE = B0 + 7 * GROUPS


def kernel(
    tok, cot, mom, pos, consts, out, upd,
    tall, gall, relay, tt, mom_s, pos_s, bases, mask_s, idx_s, gidx_s, vals_f, vals_b, abuf, pbuf, bbuf,
    ss, rs, ls,
):
    rep = lax.axis_index("rep")
    f = lax.axis_index("fsdp")
    x, q = rep // 8, lax.rem(rep, 8)
    zh, y = f // 4, lax.rem(f, 4)

    def at_y(j):
        return (rep, zh * 4 + lax.rem(y + j, 4))

    partner = (rep, lax.rem(f + 4, 8))

    def at_x(j):
        return (lax.rem(x + j, 4) * 8 + q, f)

    def at_q(j):
        return (x * 8 + lax.rem(q + j, 8), f)

    def remote(src, dst, k, device):
        return pltpu.make_async_remote_copy(
            src_ref=src, dst_ref=dst, send_sem=ss.at[k], recv_sem=rs.at[k], device_id=device, device_id_type=MESH
        )

    def tok_cols(block):
        return tok.at[:, pl.ds(pl.multiple_of(block * ROWS, 128), ROWS)]

    def cols(t):
        return pl.ds(pl.multiple_of(t * PIECE, PIECE), PIECE)

    def z_tok(j):
        src = tok_cols((1 - zh) * 4 + lax.rem(y + j, 4))
        return remote(src, tall.at[4] if j == 0 else relay.at[j - 1], ZT + j, partner)

    def z_cot(t):
        return remote(cot.at[:, cols(t)], gall.at[4, :, cols(t)], ZG + t, partner)

    def z_half(h):
        c = pl.ds(WHOLE * PIECE + h * HALF, HALF)
        return remote(cot.at[:, c], gall.at[4, :, c], ZH + h, partner)

    def y_tok(j):
        return remote(tok_cols(zh * 4 + lax.rem(y + j, 4)), tall.at[4 - j], YT + j - 1, at_y(j))

    def y_tok_partner(j):
        return remote(relay.at[j - 1], tall.at[8 - j], YTP + j - 1, at_y(j))

    def y_cot(way):
        return remote(cot, gall.at[3 - 2 * way], YG + way, at_y(1 + 2 * way))

    def y_cot_relay(way):
        half = pl.ds(96 * way, 96)
        return remote(gall.at[3 - 2 * way, half], gall.at[2, half], YGR + way, at_y(1 + 2 * way))

    def y_piece(t, way):
        return remote(gall.at[4, :, cols(t)], gall.at[7 - 2 * way, :, cols(t)], YP + 2 * t + way, at_y(1 + 2 * way))

    def y_piece_relay(t, way):
        half = pl.ds(96 * way, 96)
        return remote(
            gall.at[7 - 2 * way, half, cols(t)], gall.at[6, half, cols(t)], YPR + 2 * t + way, at_y(1 + 2 * way)
        )

    def y_half(h, j):
        c = pl.ds(WHOLE * PIECE + h * HALF, HALF)
        return remote(gall.at[4, :, c], gall.at[8 - j, :, c], YH + 3 * h + j - 1, at_y(j))

    def rep_x(b, j):
        rows = pl.ds(pl.multiple_of(lax.rem(x + j, 4) * GROUP_ROWS, 32), GROUP_ROWS)
        return remote(vals_b.at[b, rows], abuf.at[b, j - 1], A0 + 3 * b + j - 1, at_x(j))

    def window(who):
        return pl.ds(pl.multiple_of(((5 * who) // 4) * 16, 16), WINDOW)

    def rep_q(b, j):
        rows = window(lax.rem(q + j, 8))
        return remote(pbuf.at[b, rows], bbuf.at[b, j - 1], B0 + 7 * b + j - 1, at_q(j))

    def local(src, dst, k):
        return pltpu.make_async_copy(src, dst, ls.at[k])

    locals_in = [
        local(pos, pos_s, 0),
        local(cot, gall.at[0], 1),
        local(tok_cols(f), tall.at[0], 2),
        local(mom, mom_s, 3),
        local(consts, bases, 4),
    ]
    for copy in locals_in:
        copy.start()

    barrier = pltpu.get_barrier_semaphore()
    friends = [partner] + [at_y(j) for j in (1, 2, 3)] + [at_x(j) for j in (1, 2, 3)] + [at_q(j) for j in range(1, 8)]
    for friend in friends:
        pl.semaphore_signal(barrier, inc=1, device_id=friend, device_id_type=MESH)
    pl.semaphore_wait(barrier, len(friends))

    for j in (1, 2, 3):
        z_tok(j).start()
    for way in (0, 1):
        y_cot(way).start()
    for j in (1, 3, 2):
        y_tok(j).start()
    z_tok(0).start()
    for t in range(AHEAD):
        z_cot(t).start()

    locals_in[0].wait()

    def lanes(rows):
        return lax.broadcasted_iota(jnp.int32, (rows, 128), 1)

    def shift(rows):
        return SPAN * lax.rem(lanes(rows) // KEEP, 2)

    def blocks_of(b):
        return [(bb, 8 * b + bb) for bb in range(8)] if b < 2 else [(bb, 12 + bb) for bb in range(4, 8)]

    for b, first in enumerate((0, 128, 192)):
        for i in range(ROWS // 128):
            rows = slice(i * 128, (i + 1) * 128)
            idx_s[b, rows, :] = pos_s[first : first + 128, rows].T + shift(128)

    def prepare(i, carry):
        rows = pl.ds(pl.multiple_of(i * 32, 32), 32)
        lane = lanes(32)
        half = KEEP * (lane // SPAN)
        inside = lax.rem(lane, SPAN)
        for b in range(GROUPS):
            block = idx_s[b, rows, :] - shift(32)
            for bb, column in blocks_of(b):
                hit = jnp.zeros((32, 128), jnp.float32)
                for m in range(KEEP):
                    hit = jnp.where(lane_gather(block, half + (16 * bb + m)) == inside, 1.0, hit)
                mask_s[rows, column * 128 : column * 128 + 128] = hit.astype(jnp.bfloat16)
        return carry

    lax.fori_loop(0, ROWS // 32, prepare, 0)

    upwards = lax.rem(WINDOW - 4 * lax.rem(rep, 4), WINDOW)
    lane = lanes(WINDOW)
    for b in range(GROUPS):
        block = pltpu.roll(idx_s[b, window(rep), :] - shift(WINDOW), upwards, 0)
        for bb, column in blocks_of(b):
            found = jnp.full((WINDOW, 128), -1, jnp.int32)
            for m in range(KEEP):
                source = KEEP * (lane // SPAN) + (16 * bb + m)
                found = jnp.where(lane_gather(block, source) == lax.rem(lane, SPAN), source, found)
            gidx_s[:, column * 128 : column * 128 + 128] = found

    z_tok(1).wait_recv()
    y_tok_partner(1).start()
    for way in (0, 1):
        y_cot(way).wait_recv()
        y_cot_relay(way).start()
    for j in (2, 3):
        z_tok(j).wait_recv()
        y_tok_partner(j).start()

    def turn(pair):
        block = tall[2 * pair : 2 * pair + 2].reshape(2 * BLOCK, ROWS)
        tt[:, pair * 2 * BLOCK : (pair + 1) * 2 * BLOCK] = block.T

    for copy in locals_in[1:]:
        copy.wait()
    for j in (1, 2, 3):
        y_tok(j).wait_recv()
    turn(0)
    turn(1)
    z_tok(0).wait_recv()

    def compute(s):
        c = cols(s)
        gradient = mm(tt[...], gall[:, :, c].reshape(SLOTS * BLOCK, PIECE))
        updated = MOMENTUM_DECAY * mom_s[:, c].astype(jnp.float32) + gradient
        high, low = split(updated)
        coeffs = mm(high, bases[0]) + mm(low, bases[0]) + mm(high, bases[1])
        rounded = coeffs.astype(jnp.bfloat16)
        kept = rounded * mask_s[:, c]
        restored = mm(kept, bases[2]) + mm(kept, bases[3])
        out[:, c] = (updated - restored).astype(jnp.bfloat16)
        b = s // 4
        first = 2 * lax.rem(s, 4) + jnp.where(s >= 8, 4, 0)
        index = idx_s[b]
        values = vals_f[...]
        place = lanes(ROWS) // 16
        wide = rounded.astype(jnp.float32)
        for k in (0, 1):
            values = jnp.where(place == first + k, lane_gather(wide[:, k * 128 : k * 128 + 128], index), values)
        vals_f[...] = values

    def share(b):
        vals_b[b] = vals_f[...].astype(jnp.bfloat16)
        for j in (1, 2, 3):
            rep_x(b, j).start()

    def add_x(b):
        own = pl.ds(pl.multiple_of(x * GROUP_ROWS, 32), GROUP_ROWS)
        total = vals_b[b, own, :].astype(jnp.float32)
        for j in (1, 2, 3):
            rep_x(b, j).wait_recv()
            total = total + abuf[b, j - 1].astype(jnp.float32)
        pbuf[b] = total.astype(jnp.bfloat16)
        for j in range(1, 8):
            rep_q(b, j).start()

    def decode(b):
        total = pbuf[b, window(q), :].astype(jnp.float32)
        for j in range(1, 8):
            rep_q(b, j).wait_recv()
            total = total + bbuf[b, j - 1].astype(jnp.float32)
        total = pltpu.roll(total, upwards, 0)
        parts = []
        for _, column in blocks_of(b):
            found = gidx_s[:, column * 128 : column * 128 + 128]
            parts.append(jnp.where(found >= 0, lane_gather(total, jnp.maximum(found, 0)), 0.0))
        spread = jnp.concatenate(
            [jnp.concatenate(parts[k : k + 2], axis=1) for k in range(0, len(parts), 2)], axis=0
        )
        high, low = split(spread)
        restored = mm(high, bases[2]) + mm(low, bases[2]) + mm(high, bases[3])
        restored = (restored * (1.0 / math.sqrt(REPLICAS))).astype(jnp.bfloat16)
        for k in range(len(parts) // 2):
            c = slice(b * 1024 + k * PIECE, b * 1024 + (k + 1) * PIECE)
            upd[:, c] = restored[k * WINDOW : k * WINDOW + ROWS // REPLICAS]

    vals_f[...] = jnp.zeros_like(vals_f)

    def step(t, carry):
        @pl.when(t < WHOLE)
        def _():
            z_cot(t).wait_recv()
            for way in (0, 1):
                y_piece(t, way).start()

        @pl.when(t + AHEAD < WHOLE)
        def _():
            z_cot(t + AHEAD).start()

        @pl.when(t + AHEAD == WHOLE)
        def _():
            z_half(0).start()
            z_half(1).start()

        @pl.when(t == WHOLE)
        def _():
            z_half(0).wait_recv()
            for j in (1, 3, 2):
                y_half(0, j).start()

        @pl.when((t >= 1) & (t <= WHOLE))
        def _():
            for way in (0, 1):
                y_piece(t - 1, way).wait_recv()
                y_piece_relay(t - 1, way).start()

        @pl.when(t == WHOLE)
        def _():
            z_half(1).wait_recv()
            for j in (1, 3, 2):
                y_half(1, j).start()

        @pl.when(t == 2)
        def _():
            for j in (1, 2, 3):
                y_tok_partner(j).wait_recv()
            turn(2)
            turn(3)
            for way in (0, 1):
                y_cot_relay(way).wait_recv()

        def finish_piece(s, inner):
            @pl.when(s < WHOLE)
            def _():
                for way in (0, 1):
                    y_piece_relay(s, way).wait_recv()

            @pl.when(s == WHOLE)
            def _():
                for h in (0, 1):
                    for j in (1, 2, 3):
                        y_half(h, j).wait_recv()

            compute(s)
            return inner

        @pl.when(t >= 3)
        def _():
            lax.fori_loop(jnp.where(t == 3, 0, t - 2), t - 1, finish_piece, 0)

        @pl.when(t == 5)
        def _():
            share(0)

        @pl.when(t == 6)
        def _():
            add_x(0)

        @pl.when(t == 8)
        def _():
            decode(0)

        @pl.when(t == 9)
        def _():
            share(1)

        return carry

    lax.fori_loop(0, PIECES + 2, step, 0)
    share(2)
    add_x(1)
    add_x(2)
    decode(1)
    decode(2)

    for j in range(4):
        z_tok(j).wait_send()
    for j in (1, 2, 3):
        y_tok(j).wait_send()
        y_tok_partner(j).wait_send()
    for way in (0, 1):
        y_cot(way).wait_send()
        y_cot_relay(way).wait_send()

    def finish(t, carry):
        z_cot(t).wait_send()
        for way in (0, 1):
            y_piece(t, way).wait_send()
            y_piece_relay(t, way).wait_send()
        return carry

    lax.fori_loop(0, WHOLE, finish, 0)
    for h in (0, 1):
        z_half(h).wait_send()
        for j in (1, 2, 3):
            y_half(h, j).wait_send()
    for b in range(GROUPS):
        for j in (1, 2, 3):
            rep_x(b, j).wait_send()
        for j in range(1, 8):
            rep_q(b, j).wait_send()


def body(tokens, cotangent, momentum, positions):
    anywhere = pl.BlockSpec(memory_space=pl.ANY)
    near = pl.BlockSpec(memory_space=pltpu.VMEM)
    bf16, f32, i32 = jnp.bfloat16, jnp.float32, jnp.int32
    new_momentum, update = pl.pallas_call(
        kernel,
        out_shape=(
            pltpu.VMEM((ROWS, WIDTH), bf16),
            pltpu.VMEM((ROWS // REPLICAS, WIDTH), bf16),
        ),
        in_specs=[anywhere] * 5,
        out_specs=(near, near),
        scratch_shapes=[
            pltpu.VMEM((SLOTS, BLOCK, ROWS), bf16),
            pltpu.VMEM((SLOTS, BLOCK, WIDTH), bf16),
            pltpu.VMEM((3, BLOCK, ROWS), bf16),
            pltpu.VMEM((ROWS, SLOTS * BLOCK), bf16),
            pltpu.VMEM((ROWS, WIDTH), bf16),
            pltpu.VMEM((WIDTH // SPAN * KEEP, ROWS), i32),
            pltpu.VMEM((4, PIECE, PIECE), bf16),
            pltpu.VMEM((ROWS, WIDTH), bf16),
            pltpu.VMEM((GROUPS, ROWS, 128), i32),
            pltpu.VMEM((WINDOW, WIDTH), i32),
            pltpu.VMEM((ROWS, 128), f32),
            pltpu.VMEM((GROUPS, ROWS, 128), bf16),
            pltpu.VMEM((GROUPS, 3, GROUP_ROWS, 128), bf16),
            pltpu.VMEM((GROUPS, GROUP_ROWS, 128), bf16),
            pltpu.VMEM((GROUPS, 7, WINDOW, 128), bf16),
            pltpu.SemaphoreType.DMA((REMOTE,)),
            pltpu.SemaphoreType.DMA((REMOTE,)),
            pltpu.SemaphoreType.DMA((5,)),
        ],
        compiler_params=pltpu.CompilerParams(
            collective_id=0, has_side_effects=True, vmem_limit_bytes=56 * 1024 * 1024
        ),
    )(tokens, cotangent, momentum.reshape(ROWS, WIDTH), positions.T, jnp.asarray(block_bases()))
    return new_momentum.reshape(1, ROWS, WIDTH), update


def solution(mesh):
    in_specs = (
        P(("rep", "fsdp"), None),
        P(("rep", "fsdp"), None),
        P("rep", "fsdp", None),
        P("fsdp", None),
    )
    out_specs = (P("rep", "fsdp", None), P(("fsdp", "rep"), None))
    return jax.shard_map(body, mesh=mesh, in_specs=in_specs, out_specs=out_specs, check_vma=False)
```

```python
import functools
import math

import jax
import jax.numpy as jnp
import numpy as np
from jax import lax
from jax.experimental import pallas as pl
from jax.experimental.pallas import tpu as pltpu
from jax.sharding import PartitionSpec as P

SPAN = 64
KEEP = 8
MOMENTUM_DECAY = 0.9
MESH = pl.DeviceIdType.MESH

REPLICAS = 32
ROWS = 640
WIDTH = 2560
BLOCK = 192
SLOTS = 8
PIECE = 256
PIECES = WIDTH // PIECE
WHOLE = PIECES - 1
HALF = PIECE // 2
GROUPS = 3
GROUP_ROWS = ROWS // 4
WINDOW = 32
AHEAD = 3


def block_bases():
    freqs = np.arange(SPAN, dtype=np.float64)[:, None]
    places = np.arange(SPAN, dtype=np.float64)[None, :]
    weights = np.where(freqs == 0.0, math.sqrt(1.0 / SPAN), math.sqrt(2.0 / SPAN))
    basis = (weights * np.cos(math.pi * (2.0 * places + 1.0) * freqs / (2.0 * SPAN))).astype(np.float32)
    inverse = np.kron(np.eye(PIECE // SPAN, dtype=np.float32), basis)
    out = []
    for matrix in (inverse.T, inverse):
        high = matrix.astype(jnp.bfloat16)
        low = (matrix - high.astype(np.float32)).astype(jnp.bfloat16)
        out += [high, low]
    return np.stack(out)


def split(value):
    high = value.astype(jnp.bfloat16)
    return high, (value - high.astype(jnp.float32)).astype(jnp.bfloat16)


def mm(a, b):
    return jnp.dot(a, b, preferred_element_type=jnp.float32)


def lane_gather(value, index):
    return jnp.take_along_axis(value, index, axis=1, mode="promise_in_bounds")


ZT, ZG, ZH = 0, 4, 4 + WHOLE
YT = ZH + 2
YTP, YG, YGR = YT + 3, YT + 6, YT + 8
YP = YGR + 2
YPR = YP + 2 * WHOLE
YH = YPR + 2 * WHOLE
A0 = YH + 6
B0 = A0 + 3 * GROUPS
REMOTE = B0 + 7 * GROUPS


def kernel(
    tok, cot, mom, pos, consts, out, upd,
    tall, gall, relay, tt, mom_s, pos_s, bases, mask_s, idx_s, gidx_s, vals_f, vals_b, abuf, pbuf, bbuf,
    ss, rs, ls,
):
    rep = lax.axis_index("rep")
    f = lax.axis_index("fsdp")
    x, q = rep // 8, lax.rem(rep, 8)
    zh, y = f // 4, lax.rem(f, 4)

    def at_y(j):
        return (rep, zh * 4 + lax.rem(y + j, 4))

    partner = (rep, lax.rem(f + 4, 8))

    def at_x(j):
        return (lax.rem(x + j, 4) * 8 + q, f)

    def at_q(j):
        return (x * 8 + lax.rem(q + j, 8), f)

    def remote(src, dst, k, device):
        return pltpu.make_async_remote_copy(
            src_ref=src, dst_ref=dst, send_sem=ss.at[k], recv_sem=rs.at[k], device_id=device, device_id_type=MESH
        )

    def tok_cols(block):
        return tok.at[:, pl.ds(pl.multiple_of(block * ROWS, 128), ROWS)]

    def cols(t):
        return pl.ds(pl.multiple_of(t * PIECE, PIECE), PIECE)

    def z_tok(j):
        src = tok_cols((1 - zh) * 4 + lax.rem(y + j, 4))
        return remote(src, tall.at[4] if j == 0 else relay.at[j - 1], ZT + j, partner)

    def z_cot(t):
        return remote(cot.at[:, cols(t)], gall.at[4, :, cols(t)], ZG + t, partner)

    def z_half(h):
        c = pl.ds(WHOLE * PIECE + h * HALF, HALF)
        return remote(cot.at[:, c], gall.at[4, :, c], ZH + h, partner)

    def y_tok(j):
        return remote(tok_cols(zh * 4 + lax.rem(y + j, 4)), tall.at[4 - j], YT + j - 1, at_y(j))

    def y_tok_partner(j):
        return remote(relay.at[j - 1], tall.at[8 - j], YTP + j - 1, at_y(j))

    def y_cot(way):
        return remote(cot, gall.at[3 - 2 * way], YG + way, at_y(1 + 2 * way))

    def y_cot_relay(way):
        half = pl.ds(96 * way, 96)
        return remote(gall.at[3 - 2 * way, half], gall.at[2, half], YGR + way, at_y(1 + 2 * way))

    def y_piece(t, way):
        return remote(gall.at[4, :, cols(t)], gall.at[7 - 2 * way, :, cols(t)], YP + 2 * t + way, at_y(1 + 2 * way))

    def y_piece_relay(t, way):
        half = pl.ds(96 * way, 96)
        return remote(
            gall.at[7 - 2 * way, half, cols(t)], gall.at[6, half, cols(t)], YPR + 2 * t + way, at_y(1 + 2 * way)
        )

    def y_half(h, j):
        c = pl.ds(WHOLE * PIECE + h * HALF, HALF)
        return remote(gall.at[4, :, c], gall.at[8 - j, :, c], YH + 3 * h + j - 1, at_y(j))

    def rep_x(b, j):
        rows = pl.ds(pl.multiple_of(lax.rem(x + j, 4) * GROUP_ROWS, 32), GROUP_ROWS)
        return remote(vals_b.at[b, rows], abuf.at[b, j - 1], A0 + 3 * b + j - 1, at_x(j))

    def window(who):
        return pl.ds(pl.multiple_of(((5 * who) // 4) * 16, 16), WINDOW)

    def rep_q(b, j):
        rows = window(lax.rem(q + j, 8))
        return remote(pbuf.at[b, rows], bbuf.at[b, j - 1], B0 + 7 * b + j - 1, at_q(j))

    def local(src, dst, k):
        return pltpu.make_async_copy(src, dst, ls.at[k])

    locals_in = [
        local(pos, pos_s, 0),
        local(cot, gall.at[0], 1),
        local(tok_cols(f), tall.at[0], 2),
        local(mom, mom_s, 3),
        local(consts, bases, 4),
    ]
    for copy in locals_in:
        copy.start()

    barrier = pltpu.get_barrier_semaphore()
    friends = [partner] + [at_y(j) for j in (1, 2, 3)] + [at_x(j) for j in (1, 2, 3)] + [at_q(j) for j in range(1, 8)]
    for friend in friends:
        pl.semaphore_signal(barrier, inc=1, device_id=friend, device_id_type=MESH)
    pl.semaphore_wait(barrier, len(friends))

    for j in (1, 2, 3):
        z_tok(j).start()
    for way in (0, 1):
        y_cot(way).start()
    for j in (1, 3, 2):
        y_tok(j).start()
    z_tok(0).start()
    for t in range(AHEAD):
        z_cot(t).start()

    locals_in[0].wait()

    def lanes(rows):
        return lax.broadcasted_iota(jnp.int32, (rows, 128), 1)

    def shift(rows):
        return SPAN * lax.rem(lanes(rows) // KEEP, 2)

    def blocks_of(b):
        return [(bb, 8 * b + bb) for bb in range(8)] if b < 2 else [(bb, 12 + bb) for bb in range(4, 8)]

    for b, first in enumerate((0, 128, 192)):
        for i in range(ROWS // 128):
            rows = slice(i * 128, (i + 1) * 128)
            idx_s[b, rows, :] = pos_s[first : first + 128, rows].T + shift(128)

    def prepare(i, carry):
        rows = pl.ds(pl.multiple_of(i * 16, 16), 16)
        lane = lanes(16)
        half = KEEP * (lane // SPAN)
        inside = lax.rem(lane, SPAN)
        for b in range(GROUPS):
            block = idx_s[b, rows, :] - shift(16)
            for bb, column in blocks_of(b):
                hit = jnp.zeros((16, 128), jnp.float32)
                for m in range(KEEP):
                    hit = jnp.where(lane_gather(block, half + (16 * bb + m)) == inside, 1.0, hit)
                mask_s[rows, column * 128 : column * 128 + 128] = hit.astype(jnp.bfloat16)
        return carry

    lax.fori_loop(0, ROWS // 16, prepare, 0)

    upwards = lax.rem(WINDOW - 4 * lax.rem(rep, 4), WINDOW)
    lane = lanes(WINDOW)
    gidx_s[2, :, 0:512] = jnp.full((WINDOW, 512), -1, jnp.int32)
    for b in range(GROUPS):
        block = pltpu.roll(idx_s[b, window(rep), :] - shift(WINDOW), upwards, 0)
        for bb, _ in blocks_of(b):
            found = jnp.full((WINDOW, 128), -1, jnp.int32)
            for m in range(KEEP):
                source = KEEP * (lane // SPAN) + (16 * bb + m)
                found = jnp.where(lane_gather(block, source) == lax.rem(lane, SPAN), source, found)
            gidx_s[b, :, bb * 128 : bb * 128 + 128] = found

    z_tok(1).wait_recv()
    y_tok_partner(1).start()
    for way in (0, 1):
        y_cot(way).wait_recv()
        y_cot_relay(way).start()
    for j in (2, 3):
        z_tok(j).wait_recv()
        y_tok_partner(j).start()

    def turn(pair):
        block = tall[2 * pair : 2 * pair + 2].reshape(2 * BLOCK, ROWS)
        tt[:, pair * 2 * BLOCK : (pair + 1) * 2 * BLOCK] = block.T

    for copy in locals_in[1:]:
        copy.wait()
    for j in (1, 2, 3):
        y_tok(j).wait_recv()
    turn(0)
    turn(1)
    z_tok(0).wait_recv()

    def compute(s):
        c = cols(s)
        gradient = mm(tt[...], gall[:, :, c].reshape(SLOTS * BLOCK, PIECE))
        updated = MOMENTUM_DECAY * mom_s[:, c].astype(jnp.float32) + gradient
        high, low = split(updated)
        coeffs = mm(high, bases[0]) + mm(low, bases[0]) + mm(high, bases[1])
        rounded = coeffs.astype(jnp.bfloat16)
        kept = rounded * mask_s[:, c]
        restored = mm(kept, bases[2]) + mm(kept, bases[3])
        out[:, c] = (updated - restored).astype(jnp.bfloat16)
        b = s // 4
        first = 2 * lax.rem(s, 4) + jnp.where(s >= 8, 4, 0)
        index = idx_s[b]
        values = vals_f[...]
        place = lanes(ROWS) // 16
        wide = rounded.astype(jnp.float32)
        for k in (0, 1):
            values = jnp.where(place == first + k, lane_gather(wide[:, k * 128 : k * 128 + 128], index), values)
        vals_f[...] = values

    def share(b):
        vals_b[b] = vals_f[...].astype(jnp.bfloat16)
        for j in (1, 2, 3):
            rep_x(b, j).start()

    def add_x(b):
        own = pl.ds(pl.multiple_of(x * GROUP_ROWS, 32), GROUP_ROWS)
        total = vals_b[b, own, :].astype(jnp.float32)
        for j in (1, 2, 3):
            rep_x(b, j).wait_recv()
            total = total + abuf[b, j - 1].astype(jnp.float32)
        pbuf[b] = total.astype(jnp.bfloat16)
        for j in range(1, 8):
            rep_q(b, j).start()

    def decode(b):
        total = pbuf[b, window(q), :].astype(jnp.float32)
        for j in range(1, 8):
            rep_q(b, j).wait_recv()
            total = total + bbuf[b, j - 1].astype(jnp.float32)
        total = pltpu.roll(total, upwards, 0)
        parts = []
        for bb in range(8):
            found = gidx_s[b, :, bb * 128 : bb * 128 + 128]
            parts.append(jnp.where(found >= 0, lane_gather(total, jnp.maximum(found, 0)), 0.0))
        spread = jnp.concatenate(
            [jnp.concatenate(parts[k : k + 2], axis=1) for k in range(0, len(parts), 2)], axis=0
        )
        high, low = split(spread)
        restored = mm(high, bases[2]) + mm(low, bases[2]) + mm(high, bases[3])
        restored = (restored * (1.0 / math.sqrt(REPLICAS))).astype(jnp.bfloat16)
        rows = [restored[k * WINDOW : k * WINDOW + ROWS // REPLICAS] for k in range(4)]

        @pl.when(b < 2)
        def _():
            for k in (0, 1):
                upd[:, cols(4 * b + k)] = rows[k]

        for k in (2, 3):
            upd[:, cols(jnp.where(b < 2, 4 * b, 6) + k)] = rows[k]

    vals_f[...] = jnp.zeros_like(vals_f)

    def step(t, carry):
        @pl.when(t < WHOLE)
        def _():
            z_cot(t).wait_recv()
            for way in (0, 1):
                y_piece(t, way).start()

        @pl.when(t + AHEAD < WHOLE)
        def _():
            z_cot(t + AHEAD).start()

        @pl.when(t + AHEAD == WHOLE)
        def _():
            z_half(0).start()
            z_half(1).start()

        @pl.when(t == WHOLE)
        def _():
            z_half(0).wait_recv()
            for j in (1, 3, 2):
                y_half(0, j).start()

        @pl.when((t >= 1) & (t <= WHOLE))
        def _():
            for way in (0, 1):
                y_piece(t - 1, way).wait_recv()
                y_piece_relay(t - 1, way).start()

        @pl.when(t == WHOLE)
        def _():
            z_half(1).wait_recv()
            for j in (1, 3, 2):
                y_half(1, j).start()

        @pl.when(t == 2)
        def _():
            for j in (1, 2, 3):
                y_tok_partner(j).wait_recv()
            turn(2)
            turn(3)
            for way in (0, 1):
                y_cot_relay(way).wait_recv()

        def finish_piece(s, inner):
            @pl.when(s < WHOLE)
            def _():
                for way in (0, 1):
                    y_piece_relay(s, way).wait_recv()

            @pl.when(s == WHOLE)
            def _():
                for h in (0, 1):
                    for j in (1, 2, 3):
                        y_half(h, j).wait_recv()

            compute(s)
            return inner

        @pl.when((t >= 3) & (t <= PIECES + 1))
        def _():
            lax.fori_loop(jnp.where(t == 3, 0, t - 2), t - 1, finish_piece, 0)

        @pl.when((t == 5) | (t == 9) | (t == 11))
        def _():
            share(jnp.where(t == 5, 0, jnp.where(t == 9, 1, 2)))

        @pl.when((t == 6) | (t == 12) | (t == 13))
        def _():
            add_x(jnp.where(t == 6, 0, t - 11))

        @pl.when((t == 8) | (t == 14) | (t == 15))
        def _():
            decode(jnp.where(t == 8, 0, t - 13))

        return carry

    lax.fori_loop(0, PIECES + 6, step, 0)

    for j in range(4):
        z_tok(j).wait_send()
    for j in (1, 2, 3):
        y_tok(j).wait_send()
        y_tok_partner(j).wait_send()
    for way in (0, 1):
        y_cot(way).wait_send()
        y_cot_relay(way).wait_send()

    def finish(t, carry):
        z_cot(t).wait_send()
        for way in (0, 1):
            y_piece(t, way).wait_send()
            y_piece_relay(t, way).wait_send()
        return carry

    lax.fori_loop(0, WHOLE, finish, 0)
    for h in (0, 1):
        z_half(h).wait_send()
        for j in (1, 2, 3):
            y_half(h, j).wait_send()
    for b in range(GROUPS):
        for j in (1, 2, 3):
            rep_x(b, j).wait_send()
        for j in range(1, 8):
            rep_q(b, j).wait_send()


def body(tokens, cotangent, momentum, positions):
    anywhere = pl.BlockSpec(memory_space=pl.ANY)
    near = pl.BlockSpec(memory_space=pltpu.VMEM)
    bf16, f32, i32 = jnp.bfloat16, jnp.float32, jnp.int32
    new_momentum, update = pl.pallas_call(
        kernel,
        out_shape=(
            pltpu.VMEM((ROWS, WIDTH), bf16),
            pltpu.VMEM((ROWS // REPLICAS, WIDTH), bf16),
        ),
        in_specs=[anywhere] * 5,
        out_specs=(near, near),
        scratch_shapes=[
            pltpu.VMEM((SLOTS, BLOCK, ROWS), bf16),
            pltpu.VMEM((SLOTS, BLOCK, WIDTH), bf16),
            pltpu.VMEM((3, BLOCK, ROWS), bf16),
            pltpu.VMEM((ROWS, SLOTS * BLOCK), bf16),
            pltpu.VMEM((ROWS, WIDTH), bf16),
            pltpu.VMEM((WIDTH // SPAN * KEEP, ROWS), i32),
            pltpu.VMEM((4, PIECE, PIECE), bf16),
            pltpu.VMEM((ROWS, WIDTH), bf16),
            pltpu.VMEM((GROUPS, ROWS, 128), i32),
            pltpu.VMEM((GROUPS, WINDOW, 1024), i32),
            pltpu.VMEM((ROWS, 128), f32),
            pltpu.VMEM((GROUPS, ROWS, 128), bf16),
            pltpu.VMEM((GROUPS, 3, GROUP_ROWS, 128), bf16),
            pltpu.VMEM((GROUPS, GROUP_ROWS, 128), bf16),
            pltpu.VMEM((GROUPS, 7, WINDOW, 128), bf16),
            pltpu.SemaphoreType.DMA((REMOTE,)),
            pltpu.SemaphoreType.DMA((REMOTE,)),
            pltpu.SemaphoreType.DMA((5,)),
        ],
        compiler_params=pltpu.CompilerParams(
            collective_id=0, has_side_effects=True, vmem_limit_bytes=56 * 1024 * 1024
        ),
    )(tokens, cotangent, momentum.reshape(ROWS, WIDTH), positions.T, jnp.asarray(block_bases()))
    return new_momentum.reshape(1, ROWS, WIDTH), update


def solution(mesh):
    in_specs = (
        P(("rep", "fsdp"), None),
        P(("rep", "fsdp"), None),
        P("rep", "fsdp", None),
        P("fsdp", None),
    )
    out_specs = (P("rep", "fsdp", None), P(("fsdp", "rep"), None))
    return jax.shard_map(body, mesh=mesh, in_specs=in_specs, out_specs=out_specs, check_vma=False)
```

```python
import functools
import math

import jax
import jax.numpy as jnp
import numpy as np
from jax import lax
from jax.experimental import pallas as pl
from jax.experimental.pallas import tpu as pltpu
from jax.sharding import PartitionSpec as P

SPAN = 64
KEEP = 8
MOMENTUM_DECAY = 0.9
MESH = pl.DeviceIdType.MESH

REPLICAS = 32
ROWS = 640
WIDTH = 2560
BLOCK = 192
SLOTS = 8
PIECE = 256
PIECES = WIDTH // PIECE
WHOLE = PIECES - 1
HALF = PIECE // 2
GROUPS = 3
GROUP_ROWS = ROWS // 4
WINDOW = 32
AHEAD = 3


def block_bases():
    freqs = np.arange(SPAN, dtype=np.float64)[:, None]
    places = np.arange(SPAN, dtype=np.float64)[None, :]
    weights = np.where(freqs == 0.0, math.sqrt(1.0 / SPAN), math.sqrt(2.0 / SPAN))
    basis = (weights * np.cos(math.pi * (2.0 * places + 1.0) * freqs / (2.0 * SPAN))).astype(np.float32)
    inverse = np.kron(np.eye(PIECE // SPAN, dtype=np.float32), basis)
    out = []
    for matrix in (inverse.T, inverse):
        high = matrix.astype(jnp.bfloat16)
        low = (matrix - high.astype(np.float32)).astype(jnp.bfloat16)
        out += [high, low]
    return np.stack(out)


def split(value):
    high = value.astype(jnp.bfloat16)
    return high, (value - high.astype(jnp.float32)).astype(jnp.bfloat16)


def mm(a, b):
    return jnp.dot(a, b, preferred_element_type=jnp.float32)


def lane_gather(value, index):
    return jnp.take_along_axis(value, index, axis=1, mode="promise_in_bounds")


ZT, ZG, ZH = 0, 4, 4 + WHOLE
YT = ZH + 2
YTP, YG, YGR = YT + 3, YT + 6, YT + 8
YP = YGR + 2
YPR = YP + 2 * WHOLE
YH = YPR + 2 * WHOLE
A0 = YH + 6
B0 = A0 + 3 * GROUPS
REMOTE = B0 + 7 * GROUPS


def kernel(
    tok, cot, mom, pos, consts, out, upd,
    tall, gall, relay, tt, mom_s, pos_s, bases, mask_s, idx_s, gidx_s, vals_f, vals_b, abuf, pbuf, bbuf,
    ss, rs, ls,
):
    rep = lax.axis_index("rep")
    f = lax.axis_index("fsdp")
    x, q = rep // 8, lax.rem(rep, 8)
    zh, y = f // 4, lax.rem(f, 4)

    def at_y(j):
        return (rep, zh * 4 + lax.rem(y + j, 4))

    partner = (rep, lax.rem(f + 4, 8))

    def at_x(j):
        return (lax.rem(x + j, 4) * 8 + q, f)

    def at_q(j):
        return (x * 8 + lax.rem(q + j, 8), f)

    def remote(src, dst, k, device):
        return pltpu.make_async_remote_copy(
            src_ref=src, dst_ref=dst, send_sem=ss.at[k], recv_sem=rs.at[k], device_id=device, device_id_type=MESH
        )

    def tok_cols(block):
        return tok.at[:, pl.ds(pl.multiple_of(block * ROWS, 128), ROWS)]

    def cols(t):
        return pl.ds(pl.multiple_of(t * PIECE, PIECE), PIECE)

    def z_tok(j):
        src = tok_cols((1 - zh) * 4 + lax.rem(y + j, 4))
        return remote(src, tall.at[4] if j == 0 else relay.at[j - 1], ZT + j, partner)

    def z_cot(t):
        return remote(cot.at[:, cols(t)], gall.at[4, :, cols(t)], ZG + t, partner)

    def z_half(h):
        c = pl.ds(WHOLE * PIECE + h * HALF, HALF)
        return remote(cot.at[:, c], gall.at[4, :, c], ZH + h, partner)

    def y_tok(j):
        return remote(tok_cols(zh * 4 + lax.rem(y + j, 4)), tall.at[4 - j], YT + j - 1, at_y(j))

    def y_tok_partner(j):
        return remote(relay.at[j - 1], tall.at[8 - j], YTP + j - 1, at_y(j))

    def y_cot(way):
        return remote(cot, gall.at[3 - 2 * way], YG + way, at_y(1 + 2 * way))

    def y_cot_relay(way):
        half = pl.ds(96 * way, 96)
        return remote(gall.at[3 - 2 * way, half], gall.at[2, half], YGR + way, at_y(1 + 2 * way))

    def y_piece(t, way):
        return remote(gall.at[4, :, cols(t)], gall.at[7 - 2 * way, :, cols(t)], YP + 2 * t + way, at_y(1 + 2 * way))

    def y_piece_relay(t, way):
        half = pl.ds(96 * way, 96)
        return remote(
            gall.at[7 - 2 * way, half, cols(t)], gall.at[6, half, cols(t)], YPR + 2 * t + way, at_y(1 + 2 * way)
        )

    def y_half(h, j):
        c = pl.ds(WHOLE * PIECE + h * HALF, HALF)
        return remote(gall.at[4, :, c], gall.at[8 - j, :, c], YH + 3 * h + j - 1, at_y(j))

    def rep_x(b, j):
        rows = pl.ds(pl.multiple_of(lax.rem(x + j, 4) * GROUP_ROWS, 32), GROUP_ROWS)
        return remote(vals_b.at[b, rows], abuf.at[b, j - 1], A0 + 3 * b + j - 1, at_x(j))

    def window(who):
        return pl.ds(pl.multiple_of(((5 * who) // 4) * 16, 16), WINDOW)

    def rep_q(b, j):
        rows = window(lax.rem(q + j, 8))
        return remote(pbuf.at[b, rows], bbuf.at[b, j - 1], B0 + 7 * b + j - 1, at_q(j))

    def local(src, dst, k):
        return pltpu.make_async_copy(src, dst, ls.at[k])

    locals_in = [
        local(pos, pos_s, 0),
        local(cot, gall.at[0], 1),
        local(tok_cols(f), tall.at[0], 2),
        local(mom, mom_s, 3),
        local(consts, bases, 4),
    ]
    for copy in locals_in:
        copy.start()

    barrier = pltpu.get_barrier_semaphore()
    friends = [partner] + [at_y(j) for j in (1, 2, 3)] + [at_x(j) for j in (1, 2, 3)] + [at_q(j) for j in range(1, 8)]
    for friend in friends:
        pl.semaphore_signal(barrier, inc=1, device_id=friend, device_id_type=MESH)
    pl.semaphore_wait(barrier, len(friends))

    for j in (1, 2, 3, 0):
        z_tok(j).start()
    for way in (0, 1):
        y_cot(way).start()
    for j in (1, 3, 2):
        y_tok(j).start()
    for t in range(AHEAD):
        z_cot(t).start()

    locals_in[0].wait()

    def lanes(rows):
        return lax.broadcasted_iota(jnp.int32, (rows, 128), 1)

    def shift(rows):
        return SPAN * lax.rem(lanes(rows) // KEEP, 2)

    def blocks_of(b):
        return [(bb, 8 * b + bb) for bb in range(8)] if b < 2 else [(bb, 12 + bb) for bb in range(4, 8)]

    for b, first in enumerate((0, 128, 192)):
        for i in range(ROWS // 128):
            rows = slice(i * 128, (i + 1) * 128)
            idx_s[b, rows, :] = pos_s[first : first + 128, rows].T + shift(128)

    def prepare(i, carry):
        rows = pl.ds(pl.multiple_of(i * 16, 16), 16)
        lane = lanes(16)
        half = KEEP * (lane // SPAN)
        inside = lax.rem(lane, SPAN)
        for b in range(GROUPS):
            block = idx_s[b, rows, :] - shift(16)
            for bb, column in blocks_of(b):
                hit = jnp.zeros((16, 128), jnp.float32)
                for m in range(KEEP):
                    hit = jnp.where(lane_gather(block, half + (16 * bb + m)) == inside, 1.0, hit)
                mask_s[rows, column * 128 : column * 128 + 128] = hit.astype(jnp.bfloat16)
        return carry

    lax.fori_loop(0, ROWS // 16, prepare, 0)

    upwards = lax.rem(WINDOW - 4 * lax.rem(rep, 4), WINDOW)
    lane = lanes(WINDOW)
    gidx_s[2, :, 0:512] = jnp.full((WINDOW, 512), -1, jnp.int32)
    for b in range(GROUPS):
        block = pltpu.roll(idx_s[b, window(rep), :] - shift(WINDOW), upwards, 0)
        for bb, _ in blocks_of(b):
            found = jnp.full((WINDOW, 128), -1, jnp.int32)
            for m in range(KEEP):
                source = KEEP * (lane // SPAN) + (16 * bb + m)
                found = jnp.where(lane_gather(block, source) == lax.rem(lane, SPAN), source, found)
            gidx_s[b, :, bb * 128 : bb * 128 + 128] = found

    z_tok(1).wait_recv()
    y_tok_partner(1).start()
    for way in (0, 1):
        y_cot(way).wait_recv()
        y_cot_relay(way).start()
    for j in (2, 3):
        z_tok(j).wait_recv()
        y_tok_partner(j).start()

    def turn(pair):
        block = tall[2 * pair : 2 * pair + 2].reshape(2 * BLOCK, ROWS)
        tt[:, pair * 2 * BLOCK : (pair + 1) * 2 * BLOCK] = block.T

    for copy in locals_in[1:]:
        copy.wait()
    for j in (1, 2, 3):
        y_tok(j).wait_recv()
    turn(0)
    turn(1)
    z_tok(0).wait_recv()

    def compute(s):
        c = cols(s)
        gradient = mm(tt[...], gall[:, :, c].reshape(SLOTS * BLOCK, PIECE))
        updated = MOMENTUM_DECAY * mom_s[:, c].astype(jnp.float32) + gradient
        high, low = split(updated)
        coeffs = mm(high, bases[0]) + mm(low, bases[0]) + mm(high, bases[1])
        rounded = coeffs.astype(jnp.bfloat16)
        kept = rounded * mask_s[:, c]
        b = s // 4
        first = 2 * lax.rem(s, 4) + jnp.where(s >= 8, 4, 0)
        index = idx_s[b]
        values = vals_f[...]
        place = lanes(ROWS) // 16
        wide = rounded.astype(jnp.float32)
        for k in (0, 1):
            values = jnp.where(place == first + k, lane_gather(wide[:, k * 128 : k * 128 + 128], index), values)
        vals_f[...] = values

        @pl.when((s == 3) | (s == 7) | (s == 9))
        def _():
            share(b)

        restored = mm(kept, bases[2]) + mm(kept, bases[3])
        out[:, c] = (updated - restored).astype(jnp.bfloat16)

    def share(b):
        vals_b[b] = vals_f[...].astype(jnp.bfloat16)
        for j in (1, 2, 3):
            rep_x(b, j).start()

    def add_x(b):
        own = pl.ds(pl.multiple_of(x * GROUP_ROWS, 32), GROUP_ROWS)
        total = vals_b[b, own, :].astype(jnp.float32)
        for j in (1, 2, 3):
            rep_x(b, j).wait_recv()
            total = total + abuf[b, j - 1].astype(jnp.float32)
        pbuf[b] = total.astype(jnp.bfloat16)
        for j in range(1, 8):
            rep_q(b, j).start()

    def decode(b):
        total = pbuf[b, window(q), :].astype(jnp.float32)
        for j in range(1, 8):
            rep_q(b, j).wait_recv()
            total = total + bbuf[b, j - 1].astype(jnp.float32)
        total = pltpu.roll(total, upwards, 0)
        parts = []
        for bb in range(8):
            found = gidx_s[b, :, bb * 128 : bb * 128 + 128]
            parts.append(jnp.where(found >= 0, lane_gather(total, jnp.maximum(found, 0)), 0.0))
        spread = jnp.concatenate(
            [jnp.concatenate(parts[k : k + 2], axis=1) for k in range(0, len(parts), 2)], axis=0
        )
        high, low = split(spread)
        restored = mm(high, bases[2]) + mm(low, bases[2]) + mm(high, bases[3])
        restored = (restored * (1.0 / math.sqrt(REPLICAS))).astype(jnp.bfloat16)
        rows = [restored[k * WINDOW : k * WINDOW + ROWS // REPLICAS] for k in range(4)]

        @pl.when(b < 2)
        def _():
            for k in (0, 1):
                upd[:, cols(4 * b + k)] = rows[k]

        for k in (2, 3):
            upd[:, cols(jnp.where(b < 2, 4 * b, 6) + k)] = rows[k]

    vals_f[...] = jnp.zeros_like(vals_f)

    def step(t, carry):
        @pl.when(t < WHOLE)
        def _():
            z_cot(t).wait_recv()
            for way in (0, 1):
                y_piece(t, way).start()

        @pl.when(t + AHEAD < WHOLE)
        def _():
            z_cot(t + AHEAD).start()

        @pl.when(t + AHEAD == WHOLE)
        def _():
            z_half(0).start()
            z_half(1).start()

        @pl.when(t == WHOLE)
        def _():
            z_half(0).wait_recv()
            for j in (1, 3, 2):
                y_half(0, j).start()

        @pl.when((t >= 1) & (t <= WHOLE))
        def _():
            for way in (0, 1):
                y_piece(t - 1, way).wait_recv()
                y_piece_relay(t - 1, way).start()

        @pl.when(t == WHOLE)
        def _():
            z_half(1).wait_recv()
            for j in (1, 3, 2):
                y_half(1, j).start()

        @pl.when(t == 2)
        def _():
            for j in (1, 2, 3):
                y_tok_partner(j).wait_recv()
            turn(2)
            turn(3)
            for way in (0, 1):
                y_cot_relay(way).wait_recv()

        def finish_piece(s, inner):
            @pl.when(s < WHOLE)
            def _():
                for way in (0, 1):
                    y_piece_relay(s, way).wait_recv()

            @pl.when(s == WHOLE)
            def _():
                for h in (0, 1):
                    for j in (1, 2, 3):
                        y_half(h, j).wait_recv()

            compute(s)
            return inner

        @pl.when((t >= 3) & (t <= PIECES + 1))
        def _():
            lax.fori_loop(jnp.where(t == 3, 0, t - 2), t - 1, finish_piece, 0)

        @pl.when((t == 6) | (t == 12) | (t == 13))
        def _():
            add_x(jnp.where(t == 6, 0, t - 11))

        @pl.when((t == 8) | (t == 14) | (t == 15))
        def _():
            decode(jnp.where(t == 8, 0, t - 13))

        return carry

    lax.fori_loop(0, PIECES + 6, step, 0)

    for j in range(4):
        z_tok(j).wait_send()
    for j in (1, 2, 3):
        y_tok(j).wait_send()
        y_tok_partner(j).wait_send()
    for way in (0, 1):
        y_cot(way).wait_send()
        y_cot_relay(way).wait_send()

    def finish(t, carry):
        z_cot(t).wait_send()
        for way in (0, 1):
            y_piece(t, way).wait_send()
            y_piece_relay(t, way).wait_send()
        return carry

    lax.fori_loop(0, WHOLE, finish, 0)
    for h in (0, 1):
        z_half(h).wait_send()
        for j in (1, 2, 3):
            y_half(h, j).wait_send()
    for b in range(GROUPS):
        for j in (1, 2, 3):
            rep_x(b, j).wait_send()
        for j in range(1, 8):
            rep_q(b, j).wait_send()


def body(tokens, cotangent, momentum, positions):
    anywhere = pl.BlockSpec(memory_space=pl.ANY)
    near = pl.BlockSpec(memory_space=pltpu.VMEM)
    bf16, f32, i32 = jnp.bfloat16, jnp.float32, jnp.int32
    new_momentum, update = pl.pallas_call(
        kernel,
        out_shape=(
            pltpu.VMEM((ROWS, WIDTH), bf16),
            pltpu.VMEM((ROWS // REPLICAS, WIDTH), bf16),
        ),
        in_specs=[anywhere] * 5,
        out_specs=(near, near),
        scratch_shapes=[
            pltpu.VMEM((SLOTS, BLOCK, ROWS), bf16),
            pltpu.VMEM((SLOTS, BLOCK, WIDTH), bf16),
            pltpu.VMEM((3, BLOCK, ROWS), bf16),
            pltpu.VMEM((ROWS, SLOTS * BLOCK), bf16),
            pltpu.VMEM((ROWS, WIDTH), bf16),
            pltpu.VMEM((WIDTH // SPAN * KEEP, ROWS), i32),
            pltpu.VMEM((4, PIECE, PIECE), bf16),
            pltpu.VMEM((ROWS, WIDTH), bf16),
            pltpu.VMEM((GROUPS, ROWS, 128), i32),
            pltpu.VMEM((GROUPS, WINDOW, 1024), i32),
            pltpu.VMEM((ROWS, 128), f32),
            pltpu.VMEM((GROUPS, ROWS, 128), bf16),
            pltpu.VMEM((GROUPS, 3, GROUP_ROWS, 128), bf16),
            pltpu.VMEM((GROUPS, GROUP_ROWS, 128), bf16),
            pltpu.VMEM((GROUPS, 7, WINDOW, 128), bf16),
            pltpu.SemaphoreType.DMA((REMOTE,)),
            pltpu.SemaphoreType.DMA((REMOTE,)),
            pltpu.SemaphoreType.DMA((5,)),
        ],
        compiler_params=pltpu.CompilerParams(
            collective_id=0, has_side_effects=True, vmem_limit_bytes=56 * 1024 * 1024
        ),
    )(tokens, cotangent, momentum.reshape(ROWS, WIDTH), positions.T, jnp.asarray(block_bases()))
    return new_momentum.reshape(1, ROWS, WIDTH), update


def solution(mesh):
    in_specs = (
        P(("rep", "fsdp"), None),
        P(("rep", "fsdp"), None),
        P("rep", "fsdp", None),
        P("fsdp", None),
    )
    out_specs = (P("rep", "fsdp", None), P(("fsdp", "rep"), None))
    return jax.shard_map(body, mesh=mesh, in_specs=in_specs, out_specs=out_specs, check_vma=False)
```

```python
import functools
import math

import jax
import jax.numpy as jnp
import numpy as np
from jax import lax
from jax.experimental import pallas as pl
from jax.experimental.pallas import tpu as pltpu
from jax.sharding import PartitionSpec as P

SPAN = 64
KEEP = 8
MOMENTUM_DECAY = 0.9
MESH = pl.DeviceIdType.MESH

REPLICAS = 32
ROWS = 640
WIDTH = 2560
BLOCK = 192
SLOTS = 8
PIECE = 256
PIECES = WIDTH // PIECE
WHOLE = PIECES - 1
HALF = PIECE // 2
GROUPS = 3
GROUP_ROWS = ROWS // 4
WINDOW = 32
AHEAD = 3


def block_bases():
    freqs = np.arange(SPAN, dtype=np.float64)[:, None]
    places = np.arange(SPAN, dtype=np.float64)[None, :]
    weights = np.where(freqs == 0.0, math.sqrt(1.0 / SPAN), math.sqrt(2.0 / SPAN))
    basis = (weights * np.cos(math.pi * (2.0 * places + 1.0) * freqs / (2.0 * SPAN))).astype(np.float32)
    inverse = np.kron(np.eye(PIECE // SPAN, dtype=np.float32), basis)
    out = []
    for matrix in (inverse.T, inverse):
        high = matrix.astype(jnp.bfloat16)
        low = (matrix - high.astype(np.float32)).astype(jnp.bfloat16)
        out += [high, low]
    return np.stack(out)


def split(value):
    high = value.astype(jnp.bfloat16)
    return high, (value - high.astype(jnp.float32)).astype(jnp.bfloat16)


def mm(a, b):
    return jnp.dot(a, b, preferred_element_type=jnp.float32)


def lane_gather(value, index):
    return jnp.take_along_axis(value, index, axis=1, mode="promise_in_bounds")


ZT, ZG, ZH = 0, 4, 4 + WHOLE
YT = ZH + 2
YTP, YG, YGR = YT + 3, YT + 6, YT + 8
YP = YGR + 2
YPR = YP + 2 * WHOLE
YH = YPR + 2 * WHOLE
A0 = YH + 6
B0 = A0 + 3 * GROUPS
REMOTE = B0 + 7 * GROUPS


def kernel(
    tok, cot, mom, pos, consts, out, upd,
    tall, gall, relay, tt, mom_s, pos_s, bases, mask_s, idx_s, gidx_s, updated_s, vals_f, vals_b, abuf, pbuf, bbuf,
    ss, rs, ls,
):
    rep = lax.axis_index("rep")
    f = lax.axis_index("fsdp")
    x, q = rep // 8, lax.rem(rep, 8)
    zh, y = f // 4, lax.rem(f, 4)

    def at_y(j):
        return (rep, zh * 4 + lax.rem(y + j, 4))

    partner = (rep, lax.rem(f + 4, 8))

    def at_x(j):
        return (lax.rem(x + j, 4) * 8 + q, f)

    def at_q(j):
        return (x * 8 + lax.rem(q + j, 8), f)

    def remote(src, dst, k, device):
        return pltpu.make_async_remote_copy(
            src_ref=src, dst_ref=dst, send_sem=ss.at[k], recv_sem=rs.at[k], device_id=device, device_id_type=MESH
        )

    def tok_cols(block):
        return tok.at[:, pl.ds(pl.multiple_of(block * ROWS, 128), ROWS)]

    def cols(t):
        return pl.ds(pl.multiple_of(t * PIECE, PIECE), PIECE)

    def z_tok(j):
        src = tok_cols((1 - zh) * 4 + lax.rem(y + j, 4))
        return remote(src, tall.at[4] if j == 0 else relay.at[j - 1], ZT + j, partner)

    def z_cot(t):
        return remote(cot.at[:, cols(t)], gall.at[4, :, cols(t)], ZG + t, partner)

    def z_half(h):
        c = pl.ds(WHOLE * PIECE + h * HALF, HALF)
        return remote(cot.at[:, c], gall.at[4, :, c], ZH + h, partner)

    def y_tok(j):
        return remote(tok_cols(zh * 4 + lax.rem(y + j, 4)), tall.at[4 - j], YT + j - 1, at_y(j))

    def y_tok_partner(j):
        return remote(relay.at[j - 1], tall.at[8 - j], YTP + j - 1, at_y(j))

    def y_cot(way):
        return remote(cot, gall.at[3 - 2 * way], YG + way, at_y(1 + 2 * way))

    def y_cot_relay(way):
        half = pl.ds(96 * way, 96)
        return remote(gall.at[3 - 2 * way, half], gall.at[2, half], YGR + way, at_y(1 + 2 * way))

    def y_piece(t, way):
        return remote(gall.at[4, :, cols(t)], gall.at[7 - 2 * way, :, cols(t)], YP + 2 * t + way, at_y(1 + 2 * way))

    def y_piece_relay(t, way):
        half = pl.ds(96 * way, 96)
        return remote(
            gall.at[7 - 2 * way, half, cols(t)], gall.at[6, half, cols(t)], YPR + 2 * t + way, at_y(1 + 2 * way)
        )

    def y_half(h, j):
        c = pl.ds(WHOLE * PIECE + h * HALF, HALF)
        return remote(gall.at[4, :, c], gall.at[8 - j, :, c], YH + 3 * h + j - 1, at_y(j))

    def rep_x(b, j):
        rows = pl.ds(pl.multiple_of(lax.rem(x + j, 4) * GROUP_ROWS, 32), GROUP_ROWS)
        return remote(vals_b.at[b, rows], abuf.at[b, j - 1], A0 + 3 * b + j - 1, at_x(j))

    def window(who):
        return pl.ds(pl.multiple_of(((5 * who) // 4) * 16, 16), WINDOW)

    def rep_q(b, j):
        rows = window(lax.rem(q + j, 8))
        return remote(pbuf.at[b, rows], bbuf.at[b, j - 1], B0 + 7 * b + j - 1, at_q(j))

    def local(src, dst, k):
        return pltpu.make_async_copy(src, dst, ls.at[k])

    locals_in = [
        local(pos, pos_s, 0),
        local(cot, gall.at[0], 1),
        local(tok_cols(f), tall.at[0], 2),
        local(mom, mom_s, 3),
        local(consts, bases, 4),
    ]
    for copy in locals_in:
        copy.start()

    barrier = pltpu.get_barrier_semaphore()
    friends = [partner] + [at_y(j) for j in (1, 2, 3)] + [at_x(j) for j in (1, 2, 3)] + [at_q(j) for j in range(1, 8)]
    for friend in friends:
        pl.semaphore_signal(barrier, inc=1, device_id=friend, device_id_type=MESH)
    pl.semaphore_wait(barrier, len(friends))

    for j in (1, 2, 3):
        z_tok(j).start()
    for way in (0, 1):
        y_cot(way).start()
    for j in (1, 3, 2):
        y_tok(j).start()
    z_tok(0).start()
    for t in range(AHEAD):
        z_cot(t).start()

    locals_in[0].wait()

    def lanes(rows):
        return lax.broadcasted_iota(jnp.int32, (rows, 128), 1)

    def shift(rows):
        return SPAN * lax.rem(lanes(rows) // KEEP, 2)

    def blocks_of(b):
        return [(bb, 8 * b + bb) for bb in range(8)] if b < 2 else [(bb, 12 + bb) for bb in range(4, 8)]

    for b, first in enumerate((0, 128, 192)):
        for i in range(ROWS // 128):
            rows = slice(i * 128, (i + 1) * 128)
            idx_s[b, rows, :] = pos_s[first : first + 128, rows].T + shift(128)

    def prepare(i, carry):
        rows = pl.ds(pl.multiple_of(i * 16, 16), 16)
        lane = lanes(16)
        half = KEEP * (lane // SPAN)
        inside = lax.rem(lane, SPAN)
        for b in range(GROUPS):
            block = idx_s[b, rows, :] - shift(16)
            for bb, column in blocks_of(b):
                hit = jnp.zeros((16, 128), jnp.float32)
                for m in range(KEEP):
                    hit = jnp.where(lane_gather(block, half + (16 * bb + m)) == inside, 1.0, hit)
                mask_s[rows, column * 128 : column * 128 + 128] = hit.astype(jnp.bfloat16)
        return carry

    lax.fori_loop(0, ROWS // 16, prepare, 0)

    upwards = lax.rem(WINDOW - 4 * lax.rem(rep, 4), WINDOW)
    lane = lanes(WINDOW)
    gidx_s[2, :, 0:512] = jnp.full((WINDOW, 512), -1, jnp.int32)
    for b in range(GROUPS):
        block = pltpu.roll(idx_s[b, window(rep), :] - shift(WINDOW), upwards, 0)
        for bb, _ in blocks_of(b):
            found = jnp.full((WINDOW, 128), -1, jnp.int32)
            for m in range(KEEP):
                source = KEEP * (lane // SPAN) + (16 * bb + m)
                found = jnp.where(lane_gather(block, source) == lax.rem(lane, SPAN), source, found)
            gidx_s[b, :, bb * 128 : bb * 128 + 128] = found

    z_tok(1).wait_recv()
    y_tok_partner(1).start()
    for way in (0, 1):
        y_cot(way).wait_recv()
        y_cot_relay(way).start()
    for j in (2, 3):
        z_tok(j).wait_recv()
        y_tok_partner(j).start()

    def turn(pair):
        block = tall[2 * pair : 2 * pair + 2].reshape(2 * BLOCK, ROWS)
        tt[:, pair * 2 * BLOCK : (pair + 1) * 2 * BLOCK] = block.T

    for copy in locals_in[1:]:
        copy.wait()
    for j in (1, 2, 3):
        y_tok(j).wait_recv()
    turn(0)
    turn(1)
    z_tok(0).wait_recv()

    def compute(s):
        c = cols(s)
        gradient = mm(tt[...], gall[:, :, c].reshape(SLOTS * BLOCK, PIECE))
        updated_s[...] = MOMENTUM_DECAY * mom_s[:, c].astype(jnp.float32) + gradient
        b = s // 4
        first = 2 * lax.rem(s, 4) + jnp.where(s >= 8, 4, 0)
        place = lanes(ROWS // 2) // 16

        def transform(i, carry):
            rows = pl.ds(pl.multiple_of(i * (ROWS // 2), ROWS // 2), ROWS // 2)
            updated = updated_s[rows, :]
            high, low = split(updated)
            coeffs = mm(high, bases[0]) + mm(low, bases[0]) + mm(high, bases[1])
            rounded = coeffs.astype(jnp.bfloat16)
            kept = rounded * mask_s[rows, c]
            restored = mm(kept, bases[2]) + mm(kept, bases[3])
            out[rows, c] = (updated - restored).astype(jnp.bfloat16)
            index = idx_s[b, rows, :]
            values = vals_f[rows, :]
            wide = rounded.astype(jnp.float32)
            for k in (0, 1):
                values = jnp.where(place == first + k, lane_gather(wide[:, k * 128 : k * 128 + 128], index), values)
            vals_f[rows, :] = values
            return carry

        lax.fori_loop(0, 2, transform, 0)

    def share(b):
        vals_b[b] = vals_f[...].astype(jnp.bfloat16)
        for j in (1, 2, 3):
            rep_x(b, j).start()

    def add_x(b):
        own = pl.ds(pl.multiple_of(x * GROUP_ROWS, 32), GROUP_ROWS)
        total = vals_b[b, own, :].astype(jnp.float32)
        for j in (1, 2, 3):
            rep_x(b, j).wait_recv()
            total = total + abuf[b, j - 1].astype(jnp.float32)
        pbuf[b] = total.astype(jnp.bfloat16)
        for j in range(1, 8):
            rep_q(b, j).start()

    def decode(b):
        total = pbuf[b, window(q), :].astype(jnp.float32)
        for j in range(1, 8):
            rep_q(b, j).wait_recv()
            total = total + bbuf[b, j - 1].astype(jnp.float32)
        total = pltpu.roll(total, upwards, 0)
        parts = []
        for bb in range(8):
            found = gidx_s[b, :, bb * 128 : bb * 128 + 128]
            parts.append(jnp.where(found >= 0, lane_gather(total, jnp.maximum(found, 0)), 0.0))
        spread = jnp.concatenate(
            [jnp.concatenate(parts[k : k + 2], axis=1) for k in range(0, len(parts), 2)], axis=0
        )
        high, low = split(spread)
        restored = mm(high, bases[2]) + mm(low, bases[2]) + mm(high, bases[3])
        restored = (restored * (1.0 / math.sqrt(REPLICAS))).astype(jnp.bfloat16)
        rows = [restored[k * WINDOW : k * WINDOW + ROWS // REPLICAS] for k in range(4)]

        @pl.when(b < 2)
        def _():
            for k in (0, 1):
                upd[:, cols(4 * b + k)] = rows[k]

        for k in (2, 3):
            upd[:, cols(jnp.where(b < 2, 4 * b, 6) + k)] = rows[k]

    vals_f[...] = jnp.zeros_like(vals_f)

    def step(t, carry):
        @pl.when(t < WHOLE)
        def _():
            z_cot(t).wait_recv()
            for way in (0, 1):
                y_piece(t, way).start()

        @pl.when(t + AHEAD < WHOLE)
        def _():
            z_cot(t + AHEAD).start()

        @pl.when(t + AHEAD == WHOLE)
        def _():
            z_half(0).start()
            z_half(1).start()

        @pl.when(t == WHOLE)
        def _():
            z_half(0).wait_recv()
            for j in (1, 3, 2):
                y_half(0, j).start()

        @pl.when((t >= 1) & (t <= WHOLE))
        def _():
            for way in (0, 1):
                y_piece(t - 1, way).wait_recv()
                y_piece_relay(t - 1, way).start()

        @pl.when(t == WHOLE)
        def _():
            z_half(1).wait_recv()
            for j in (1, 3, 2):
                y_half(1, j).start()

        @pl.when(t == 2)
        def _():
            for j in (1, 2, 3):
                y_tok_partner(j).wait_recv()
            turn(2)
            turn(3)
            for way in (0, 1):
                y_cot_relay(way).wait_recv()

        def finish_piece(s, inner):
            @pl.when(s < WHOLE)
            def _():
                for way in (0, 1):
                    y_piece_relay(s, way).wait_recv()

            @pl.when(s == WHOLE)
            def _():
                for h in (0, 1):
                    for j in (1, 2, 3):
                        y_half(h, j).wait_recv()

            compute(s)
            return inner

        @pl.when((t >= 3) & (t <= PIECES + 1))
        def _():
            lax.fori_loop(jnp.where(t == 3, 0, t - 2), t - 1, finish_piece, 0)

        @pl.when((t == 5) | (t == 9) | (t == 11))
        def _():
            share(jnp.where(t == 5, 0, jnp.where(t == 9, 1, 2)))

        @pl.when((t == 6) | (t == 12) | (t == 13))
        def _():
            add_x(jnp.where(t == 6, 0, t - 11))

        @pl.when((t == 8) | (t == 14) | (t == 15))
        def _():
            decode(jnp.where(t == 8, 0, t - 13))

        return carry

    lax.fori_loop(0, PIECES + 6, step, 0)

    for j in range(4):
        z_tok(j).wait_send()
    for j in (1, 2, 3):
        y_tok(j).wait_send()
        y_tok_partner(j).wait_send()
    for way in (0, 1):
        y_cot(way).wait_send()
        y_cot_relay(way).wait_send()

    def finish(t, carry):
        z_cot(t).wait_send()
        for way in (0, 1):
            y_piece(t, way).wait_send()
            y_piece_relay(t, way).wait_send()
        return carry

    lax.fori_loop(0, WHOLE, finish, 0)
    for h in (0, 1):
        z_half(h).wait_send()
        for j in (1, 2, 3):
            y_half(h, j).wait_send()
    def shared(b, carry):
        for j in (1, 2, 3):
            rep_x(b, j).wait_send()
        for j in range(1, 8):
            rep_q(b, j).wait_send()
        return carry

    lax.fori_loop(0, GROUPS, shared, 0)


def body(tokens, cotangent, momentum, positions):
    anywhere = pl.BlockSpec(memory_space=pl.ANY)
    near = pl.BlockSpec(memory_space=pltpu.VMEM)
    bf16, f32, i32 = jnp.bfloat16, jnp.float32, jnp.int32
    new_momentum, update = pl.pallas_call(
        kernel,
        out_shape=(
            pltpu.VMEM((ROWS, WIDTH), bf16),
            pltpu.VMEM((ROWS // REPLICAS, WIDTH), bf16),
        ),
        in_specs=[anywhere] * 5,
        out_specs=(near, near),
        scratch_shapes=[
            pltpu.VMEM((SLOTS, BLOCK, ROWS), bf16),
            pltpu.VMEM((SLOTS, BLOCK, WIDTH), bf16),
            pltpu.VMEM((3, BLOCK, ROWS), bf16),
            pltpu.VMEM((ROWS, SLOTS * BLOCK), bf16),
            pltpu.VMEM((ROWS, WIDTH), bf16),
            pltpu.VMEM((WIDTH // SPAN * KEEP, ROWS), i32),
            pltpu.VMEM((4, PIECE, PIECE), bf16),
            pltpu.VMEM((ROWS, WIDTH), bf16),
            pltpu.VMEM((GROUPS, ROWS, 128), i32),
            pltpu.VMEM((GROUPS, WINDOW, 1024), i32),
            pltpu.VMEM((ROWS, PIECE), f32),
            pltpu.VMEM((ROWS, 128), f32),
            pltpu.VMEM((GROUPS, ROWS, 128), bf16),
            pltpu.VMEM((GROUPS, 3, GROUP_ROWS, 128), bf16),
            pltpu.VMEM((GROUPS, GROUP_ROWS, 128), bf16),
            pltpu.VMEM((GROUPS, 7, WINDOW, 128), bf16),
            pltpu.SemaphoreType.DMA((REMOTE,)),
            pltpu.SemaphoreType.DMA((REMOTE,)),
            pltpu.SemaphoreType.DMA((5,)),
        ],
        compiler_params=pltpu.CompilerParams(
            collective_id=0, has_side_effects=True, vmem_limit_bytes=56 * 1024 * 1024
        ),
    )(tokens, cotangent, momentum.reshape(ROWS, WIDTH), positions.T, jnp.asarray(block_bases()))
    return new_momentum.reshape(1, ROWS, WIDTH), update


def solution(mesh):
    in_specs = (
        P(("rep", "fsdp"), None),
        P(("rep", "fsdp"), None),
        P("rep", "fsdp", None),
        P("fsdp", None),
    )
    out_specs = (P("rep", "fsdp", None), P(("fsdp", "rep"), None))
    return jax.shard_map(body, mesh=mesh, in_specs=in_specs, out_specs=out_specs, check_vma=False)
```
